256 devices in a mesh: row: 16 (over z, x_hi), col: 4 (over y), grp: 4 (over x_lo, core).
Axes of the slice: x: 4 (x_hi: 2, x_lo: 2; x = x_hi * 2 + x_lo), y: 4, z: 8, core: 2. Of those that a mesh axis runs over, the one named last changes fastest.
Arguments:
- act: bfloat16 [32, 1024, 768], P('grp', 'row'), may hold values from -6 to 6
- cond: bfloat16 [32, 1024, 384], P('grp', 'row'), may hold values from -6 to 6
- pair: bfloat16 [1024, 1024, 128], P('row', ('col', 'grp')), may hold values from -6 to 6
- pair_gain: float32 [128], replicated, may hold values from 0.5 to 2
- chain_ids: int32 [1024], replicated, may hold values from 0 to 2, as said below
- bias_proj: bfloat16 [128, 16], replicated, may hold values from -24 to 24
- chain_bias: float32 [2, 16], replicated, may hold values from -4 to 4
- cond_gain: float32 [384], replicated, may hold values from 0.5 to 2
- ada_scale: bfloat16 [2, 384, 768], replicated, may hold values from -0.3125 to 0.3125
- ada_shift: bfloat16 [2, 384, 768], replicated, may hold values from -0.3125 to 0.3125
- qkvg: bfloat16 [768, 4, 768], P(None, None, 'col'), may hold values from -0.21875 to 0.21875
- attn_out: bfloat16 [768, 768], P('col'), may hold values from -0.21875 to 0.21875
- out_gate: bfloat16 [2, 384, 768], replicated, may hold values from -0.3125 to 0.3125
- trans_in: bfloat16 [768, 2, 1536], P(None, None, 'col'), may hold values from -0.21875 to 0.21875
- trans_out: bfloat16 [1536, 768], P('col'), may hold values from -0.15625 to 0.15625
Outputs:
- updated: bfloat16 [32, 1024, 768], P('grp', 'row')
The draws below stay inside these ranges and needn't reach their ends.
Inputs may be any that keep to these rules, and one draw needn't show every extreme that they name: `chain_ids`: chain numbers never fall along the tokens; each of the three chains holds at least one token.
All inputs are finite; a program needn't handle non-finite values.
Results may differ from the reference program's by a relative error of at most 0.017.
The reference program's roundings to bfloat16 on the way count: a program that leaves them out, or rounds other values in their place, can miss the bound.
Values may be sent and summed in bfloat16 or wider, within the bound.
No kernel may reach another device: no remote copies, remote signals or barrier semaphores. Data moves between devices by JAX's collectives and lax.ppermute only.
A program may use at most 128 MiB of HBM per device.

```python
import math
import jax
import jax.numpy as jnp
from jax import lax

D = 768
HEADS = 16
HD = 48
CS = 384
CZ = 128
FF = 1536
N = 1024
SAMPLES = 32


def draw_chain_ids(key, part):
    key = jax.random.fold_in(key, 5)
    first_key, second_key = jax.random.split(key)
    first_cut = jax.random.randint(first_key, (), 1, N // 2 + 1)
    second_cut = jax.random.randint(second_key, (), first_cut + 1, N)
    positions = jnp.arange(N, dtype=jnp.int32)
    return ((positions >= first_cut).astype(jnp.int32) + (positions >= second_cut).astype(jnp.int32)).astype(jnp.int32)


def draw_bias_proj(key, part):
    key = jax.random.fold_in(key, 1)
    weights_drawn = jax.random.normal(key, (CZ, HEADS), jnp.float32) * CZ ** (-0.5)
    return jnp.clip(weights_drawn, -24.0, 24.0).astype(jnp.bfloat16)


def levels(key, extent, cuts, smallest, top_value):
    gain, own = 1.0, jax.random.fold_in(key, 6)
    for axis_at, parts in cuts:
        heights = jnp.exp(jax.random.uniform(jax.random.fold_in(own, axis_at), (parts,), jnp.float32, smallest / len(cuts), top_value / len(cuts)))
        gain = gain * jnp.repeat(heights, extent[axis_at] // parts).reshape([-1 if axis == axis_at else 1 for axis in range(len(extent))])
    return gain


def centred(rng, dims, width, bound, shards=(), kind=jnp.bfloat16):
    gain = levels(rng, dims, shards, -0.22, 0.18) if shards else 1.0
    result = jax.random.normal(rng, dims, jnp.float32) * width * gain
    return jnp.minimum(jnp.maximum(result, -bound), bound).astype(kind)


def setup_inputs(seed: int = 0) -> dict:
    keys = jax.random.split(jax.random.key(seed), 16)
    act = centred(keys[0], (SAMPLES, N, D), 1.0, 6.0, ((0, 4), (1, 16)))
    cond = centred(keys[1], (SAMPLES, N, CS), 1.0, 6.0, ((0, 4), (1, 16)))
    pair = centred(keys[2], (N, N, CZ), 1.0, 6.0, ((0, 16), (1, 16)))
    pair_gain = jnp.clip(jnp.exp(jax.random.uniform(keys[3], (CZ,), jnp.float32, math.log(0.5), math.log(2.0))), 0.5, 2.0)
    chain_ids = draw_chain_ids(jax.random.fold_in(keys[15], 71), 0)
    bias_proj = draw_bias_proj(jax.random.fold_in(keys[15], 71), 0)
    chain_bias = centred(keys[6], (2, HEADS), 1.0, 4.0, (), jnp.float32)
    cond_gain = jnp.clip(jnp.exp(jax.random.uniform(keys[7], (CS,), jnp.float32, math.log(0.5), math.log(2.0))), 0.5, 2.0)
    ada_scale = centred(keys[8], (2, CS, D), CS ** -0.5, 0.3125)
    ada_shift = centred(keys[9], (2, CS, D), CS ** -0.5, 0.3125)
    qkvg = centred(keys[10], (D, 4, HEADS * HD), D ** -0.5, 0.21875, ((2, 4),))
    attn_out = centred(keys[11], (HEADS * HD, D), (HEADS * HD) ** -0.5, 0.21875, ((0, 4),))
    out_gate = centred(keys[12], (2, CS, D), CS ** -0.5, 0.3125)
    trans_in = centred(keys[13], (D, 2, FF), D ** -0.5, 0.21875, ((2, 4),))
    trans_out = centred(keys[14], (FF, D), FF ** -0.5, 0.15625, ((0, 4),))
    return {"act": act, "cond": cond, "pair": pair, "pair_gain": pair_gain, "chain_ids": chain_ids, "bias_proj": bias_proj, "chain_bias": chain_bias, "cond_gain": cond_gain, "ada_scale": ada_scale, "ada_shift": ada_shift, "qkvg": qkvg, "attn_out": attn_out, "out_gate": out_gate, "trans_in": trans_in, "trans_out": trans_out}


def norm_last(values_in):
    center = values_in - lax.optimization_barrier(jnp.mean(values_in, axis=-1, keepdims=True))
    spread = lax.optimization_barrier(jnp.mean(center * center, axis=-1, keepdims=True))
    return center * lax.rsqrt(spread + 1e-05)

def reference(act, cond, pair, pair_gain, chain_ids, bias_proj, chain_bias, cond_gain, ada_scale, ada_shift, qkvg, attn_out, out_gate, trans_in, trans_out):
    cond_norm = (norm_last(cond.astype(jnp.float32)) * cond_gain).astype(jnp.bfloat16).reshape(-1, CS)
    act_norm = norm_last(act.astype(jnp.float32)).reshape(-1, D)

    def condition(weight):
        return jnp.dot(cond_norm, weight, preferred_element_type=jnp.float32)
    att_input = (jax.nn.sigmoid(condition(ada_scale[0])) * act_norm + condition(ada_shift[0])).astype(jnp.bfloat16)
    trans_input = (jax.nn.sigmoid(condition(ada_scale[1])) * act_norm + condition(ada_shift[1])).astype(jnp.bfloat16)
    projected = jnp.dot(att_input, qkvg.reshape(D, 4 * HEADS * HD), preferred_element_type=jnp.float32).reshape(-1, 4, HEADS * HD)
    queries = projected[:, 0].astype(jnp.bfloat16).reshape(SAMPLES, N, HEADS, HD)
    keys_all = projected[:, 1].astype(jnp.bfloat16).reshape(SAMPLES, N, HEADS, HD)
    values_all = projected[:, 2].astype(jnp.bfloat16).reshape(SAMPLES, N, HEADS, HD)
    gates = jax.nn.sigmoid(projected[:, 3])

    def bias_row(pair_row):
        normed = (norm_last(pair_row.astype(jnp.float32)) * pair_gain).astype(jnp.bfloat16)
        return jnp.dot(normed, bias_proj, preferred_element_type=jnp.float32).astype(jnp.bfloat16)
    pair_bias = jnp.transpose(lax.map(bias_row, pair), (2, 0, 1))
    same_chain = (chain_ids[:, None] == chain_ids[None, :]).astype(jnp.float32)
    total_bias = pair_bias.astype(jnp.float32) + chain_bias[0][:, None, None] + (chain_bias[1] - chain_bias[0])[:, None, None] * same_chain[None]
    scale = HD ** (-0.5)

    def attend(inputs):
        query_one, key_one, value_one = inputs
        scores = jnp.einsum('qhd,khd->hqk', query_one.astype(jnp.float32), key_one.astype(jnp.float32)) * scale + total_bias
        top = lax.optimization_barrier(jnp.max(scores, axis=-1, keepdims=True))
        weights = jnp.exp(scores - top)
        denom = lax.optimization_barrier(jnp.sum(weights, axis=-1))
        rounded = lax.optimization_barrier(weights.astype(jnp.bfloat16)).astype(jnp.float32)
        summed = jnp.einsum('hqk,khd->qhd', rounded, value_one.astype(jnp.float32))
        return summed / jnp.transpose(denom)[:, :, None]
    attended = lax.map(attend, (queries, keys_all, values_all)).reshape(-1, HEADS * HD)
    mixed = (gates * attended).astype(jnp.bfloat16)
    attn_part = jnp.dot(mixed, attn_out, preferred_element_type=jnp.float32)
    inner = jnp.dot(trans_input, trans_in.reshape(D, 2 * FF), preferred_element_type=jnp.float32).reshape(-1, 2, FF)
    hidden = (jax.nn.silu(inner[:, 0]) * inner[:, 1]).astype(jnp.bfloat16)
    trans_part = jnp.dot(hidden, trans_out, preferred_element_type=jnp.float32)
    updated = jax.nn.sigmoid(condition(out_gate[0])) * attn_part + jax.nn.sigmoid(condition(out_gate[1])) * trans_part
    return updated.reshape(SAMPLES, N, D).astype(jnp.bfloat16)
```

```python
import jax
import jax.numpy as jnp
from jax import lax
from jax.experimental import pallas as pl
from jax.experimental.pallas import tpu as pltpu
from jax.sharding import PartitionSpec as P

HD = 48
BF = jnp.bfloat16
F32 = jnp.float32
NT = (((1,), (1,)), ((), ()))
TN = (((0,), (0,)), ((), ()))


def dot(left, right, dims=(((1,), (0,)), ((), ()))):
    return lax.dot_general(left, right, dims, preferred_element_type=F32)


def norm_last(values_in):
    center = values_in - jnp.mean(values_in, axis=-1, keepdims=True)
    spread = jnp.mean(center * center, axis=-1, keepdims=True)
    return center * lax.rsqrt(spread + 1e-05)


def params(mib=48):
    return pltpu.CompilerParams(vmem_limit_bytes=mib * 1024 * 1024)


def cost(flops, moved, exps=0):
    return pl.CostEstimate(flops=flops, bytes_accessed=moved, transcendentals=exps)


def whole(shape):
    zeros = (0,) * len(shape)
    return pl.BlockSpec(shape, lambda *_: zeros)


def tile_bias_kernel(pair_ref, gain_ref, proj_ref, out_ref):
    half, pairs, keys, width = pair_ref.shape
    rows = jnp.swapaxes(pair_ref[...].astype(F32), 0, 1).reshape(half * pairs * keys, width)
    normed = (norm_last(rows) * gain_ref[...]).astype(BF)
    heads = lax.dot_general(
        proj_ref[...], normed, (((0,), (1,)), ((), ())), preferred_element_type=F32
    )
    lanes = half * keys
    slabs = [heads[:, p * lanes : (p + 1) * lanes][:, None, :] for p in range(pairs)]
    out_ref[...] = jnp.concatenate(slabs, axis=1).astype(BF)


def tile_bias(pair, gain, proj):
    queries, keys, width = pair.shape
    heads = proj.shape[1]
    split = pair.reshape(2, queries // 2, keys, width)
    step = 16
    return pl.pallas_call(
        tile_bias_kernel,
        grid=(queries // 2 // step,),
        in_specs=[
            pl.BlockSpec((2, step, keys, width), lambda i: (0, i, 0, 0)),
            whole((1, width)),
            whole((width, heads)),
        ],
        out_specs=pl.BlockSpec((heads, step, 2 * keys), lambda i: (0, i, 0)),
        out_shape=jax.ShapeDtypeStruct((heads, queries // 2, 2 * keys), BF),
        compiler_params=params(),
        cost_estimate=cost(2 * queries * keys * width * heads, queries * keys * width * 2),
        name="tile_bias",
    )(split, gain.reshape(1, width), proj)


def spread_bias_kernel(in_ref, out_ref):
    cols, heads, pairs, lanes = in_ref.shape
    keys = lanes // 2
    copies = out_ref.shape[0] // heads
    for head in range(heads):
        parts = [in_ref[c, head] for c in range(cols)]
        low = jnp.concatenate([p[:, :keys] for p in parts], axis=1)
        high = jnp.concatenate([p[:, keys:] for p in parts], axis=1)
        for copy in range(copies):
            out_ref[head * copies + copy, :pairs] = low
            out_ref[head * copies + copy, pairs:] = high


def spread_bias(tiles, dests):
    cols, heads, pairs, lanes = tiles.shape
    shape = (dests, 2 * pairs, cols * lanes // 2)
    return pl.pallas_call(
        spread_bias_kernel,
        in_specs=[whole(tiles.shape)],
        out_specs=whole(shape),
        grid=(1,),
        out_shape=jax.ShapeDtypeStruct(shape, BF),
        compiler_params=params(),
        cost_estimate=cost(0, tiles.size * 2 + 2 * dests * pairs * cols * lanes),
        name="spread_bias",
    )(tiles)


def project_kernel(act_ref, cond_ref, gain_ref, scale_ref, shift_ref, w_ref, qkv_ref, gate_ref, cn_ref):
    heads, pairs, _, lanes = qkv_ref.shape
    cond_norm = (norm_last(cond_ref[...].astype(F32)) * gain_ref[...]).astype(BF)
    cn_ref[...] = cond_norm
    act_norm = norm_last(act_ref[...].astype(F32))
    att = (
        jax.nn.sigmoid(dot(cond_norm, scale_ref[0])) * act_norm + dot(cond_norm, shift_ref[0])
    ).astype(BF)
    part = heads * HD
    for which in range(3):
        result = dot(w_ref[which], att, NT).astype(BF)
        for head in range(heads):
            for p in range(pairs):
                qkv_ref[head, p, which * HD : (which + 1) * HD, :] = result[
                    head * HD : (head + 1) * HD, p * lanes : (p + 1) * lanes
                ]
    gate_ref[...] = jax.nn.sigmoid(dot(w_ref[3], att, NT))


def project(act, cond, gain, scale, shift, w):
    rows, width = act.shape
    cwidth = cond.shape[1]
    part = w.shape[1]
    heads = part // HD
    step = 256
    lanes = 128
    pairs = rows // lanes
    return pl.pallas_call(
        project_kernel,
        grid=(rows // step,),
        in_specs=[
            pl.BlockSpec((step, width), lambda i: (i, 0)),
            pl.BlockSpec((step, cwidth), lambda i: (i, 0)),
            whole((1, cwidth)),
            whole((1, cwidth, width)),
            whole((1, cwidth, width)),
            whole(w.shape),
        ],
        out_specs=[
            pl.BlockSpec((heads, step // lanes, 3 * HD, lanes), lambda i: (0, i, 0, 0)),
            pl.BlockSpec((part, step), lambda i: (0, i)),
            pl.BlockSpec((step, cwidth), lambda i: (i, 0)),
        ],
        out_shape=[
            jax.ShapeDtypeStruct((heads, pairs, 3 * HD, lanes), BF),
            jax.ShapeDtypeStruct((part, rows), F32),
            jax.ShapeDtypeStruct((rows, cwidth), BF),
        ],
        compiler_params=params(),
        cost_estimate=cost(
            2 * rows * width * (2 * cwidth + 4 * part), 4 * cwidth * width + 8 * width * part
        ),
        name="project",
    )(act, cond, gain.reshape(1, cwidth), scale, shift, w)


def transition_kernel(act_ref, cn_ref, scale_ref, shift_ref, og_ref, win_ref, wout_ref, part_ref, g0_ref, g1_ref):
    cond_norm = cn_ref[...]
    act_norm = norm_last(act_ref[...].astype(F32))
    tin = (
        jax.nn.sigmoid(dot(cond_norm, scale_ref[0])) * act_norm + dot(cond_norm, shift_ref[0])
    ).astype(BF)
    inner = dot(tin, win_ref[...])
    units = wout_ref.shape[0]
    first = inner[:, :units]
    hidden = (first * jax.nn.sigmoid(first) * inner[:, units:]).astype(BF)
    part_ref[...] = dot(hidden, wout_ref[...]).astype(BF)
    g0_ref[...] = jax.nn.sigmoid(dot(cond_norm, og_ref[0]))
    g1_ref[...] = jax.nn.sigmoid(dot(cond_norm, og_ref[1]))


def transition(act, cond_norm, scale, shift, out_gate, w_in, w_out):
    rows, width = act.shape
    cwidth = cond_norm.shape[1]
    step = 256
    second = pl.BlockSpec((1, cwidth, width), lambda i: (1, 0, 0))
    row_block = pl.BlockSpec((step, width), lambda i: (i, 0))
    return pl.pallas_call(
        transition_kernel,
        grid=(rows // step,),
        in_specs=[
            row_block,
            pl.BlockSpec((step, cwidth), lambda i: (i, 0)),
            second,
            second,
            whole(out_gate.shape),
            whole(w_in.shape),
            whole(w_out.shape),
        ],
        out_specs=[row_block, row_block, row_block],
        out_shape=[
            jax.ShapeDtypeStruct((rows, width), BF),
            jax.ShapeDtypeStruct((rows, width), F32),
            jax.ShapeDtypeStruct((rows, width), F32),
        ],
        compiler_params=params(),
        cost_estimate=cost(
            2 * rows * (4 * cwidth * width + w_in.size + w_out.size),
            8 * cwidth * width + 2 * w_in.size + 2 * w_out.size + rows * width * 12,
        ),
        name="transition",
    )(act, cond_norm, scale, shift, out_gate, w_in, w_out)


def attention_kernel(place_ref, chain_ref, qkv_ref, b0, b1, b2, b3, qid_ref, kid_ref, out_ref, k_ref, v_ref):
    samples, pieces, _, span = k_ref.shape
    half = qkv_ref.shape[2] // samples
    cols = span // half
    mine = place_ref[0]

    @pl.when(pl.program_id(0) == 0)
    def _():
        for piece in range(pieces):
            for s in range(samples):
                lanes = slice(s * half, (s + 1) * half)
                blocks = [qkv_ref[c * pieces + (mine ^ piece)] for c in range(cols)]
                k_ref[s, piece] = jnp.concatenate([b[HD : 2 * HD, lanes] for b in blocks], axis=1)
                v_ref[s, piece] = jnp.concatenate([b[2 * HD :, lanes] for b in blocks], axis=1)

    step = pl.program_id(0)
    other, same = chain_ref[0], chain_ref[1]
    qid = qid_ref[...]
    totals = []
    for piece, ref in enumerate((b0, b1, b2, b3)):
        bias = ref[...].reshape(2 * half, span).astype(F32)
        totals.append(bias + jnp.where(qid == kid_ref[mine ^ piece], same, other))
    scale = HD ** (-0.5)
    results = []
    first, second = qkv_ref[2 * step], qkv_ref[2 * step + 1]
    for s in range(samples):
        lanes = slice(s * half, (s + 1) * half)
        query = jnp.concatenate([first[:HD, lanes], second[:HD, lanes]], axis=1)
        scores = [
            lax.dot_general(query, k_ref[s, p], TN, preferred_element_type=F32) * scale + totals[p]
            for p in range(pieces)
        ]
        top = jnp.max(
            jnp.maximum(jnp.maximum(scores[0], scores[1]), jnp.maximum(scores[2], scores[3])),
            axis=1,
            keepdims=True,
        )
        weights = [jnp.exp(x - top) for x in scores]
        total = jnp.sum(
            (weights[0] + weights[1]) + (weights[2] + weights[3]), axis=1, keepdims=True
        )
        summed = sum(
            dot(weights[p].astype(BF), v_ref[s, p], NT) for p in range(pieces)
        )
        results.append(jnp.transpose(summed / total).astype(BF))
    out_ref[0] = jnp.concatenate([r[:, :half] for r in results], axis=1)
    out_ref[1] = jnp.concatenate([r[:, half:] for r in results], axis=1)


def attention(place, chain, qkv, biases, qid, kid):
    blocks, rows, lanes = qkv.shape
    half = lanes // 2
    span = biases[0].shape[2]
    bias_spec = pl.BlockSpec((2, half, span), lambda i: (i, 0, 0))
    tokens = blocks * half
    return pl.pallas_call(
        attention_kernel,
        grid=(blocks // 2,),
        in_specs=[
            pl.BlockSpec(memory_space=pltpu.SMEM),
            pl.BlockSpec(memory_space=pltpu.SMEM),
            whole(qkv.shape),
            bias_spec,
            bias_spec,
            bias_spec,
            bias_spec,
            pl.BlockSpec((2 * half, 1), lambda i: (i, 0)),
            whole(kid.shape),
        ],
        out_specs=pl.BlockSpec((2, HD, lanes), lambda i: (i, 0, 0)),
        out_shape=jax.ShapeDtypeStruct((blocks, HD, lanes), BF),
        scratch_shapes=[
            pltpu.VMEM((2, 4, HD, span), BF),
            pltpu.VMEM((2, 4, HD, span), BF),
        ],
        compiler_params=params(),
        cost_estimate=cost(8 * tokens * tokens * HD, 3_000_000, 2 * tokens * tokens),
        name="attention",
    )(place, chain, qkv, *biases, qid, kid)


def mix_kernel(gate_ref, o_ref, out_ref):
    dests, _, lanes = o_ref.shape
    pairs = out_ref.shape[1] // lanes
    for r in range(dests):
        rows = slice(r // pairs * HD, (r // pairs + 1) * HD)
        cols = slice(r % pairs * lanes, (r % pairs + 1) * lanes)
        out_ref[rows, cols] = (gate_ref[rows, cols] * o_ref[r].astype(F32)).astype(BF)


def mix(gates, attended):
    return pl.pallas_call(
        mix_kernel,
        grid=(1,),
        in_specs=[whole(gates.shape), whole(attended.shape)],
        out_specs=whole(gates.shape),
        out_shape=jax.ShapeDtypeStruct(gates.shape, BF),
        compiler_params=params(),
        cost_estimate=cost(gates.size, gates.size * 8),
        name="mix",
    )(gates, attended)


def finish_kernel(col_ref, m0, m1, m2, m3, w_ref, g0_ref, g1_ref, trans_ref, out_ref):
    mine = col_ref[0]
    total = None
    for shift, ref in enumerate((m0, m1, m2, m3)):
        term = lax.dot_general(
            ref[...], w_ref[(mine + shift) % 4], TN, preferred_element_type=F32
        )
        total = term if total is None else total + term
    out_ref[...] = (g0_ref[...] * total + g1_ref[...] * trans_ref[...].astype(F32)).astype(BF)


def finish(col, mixed, w, g0, g1, trans):
    rows, width = trans.shape
    part = mixed[0].shape[0]
    step = 256
    row_block = pl.BlockSpec((step, width), lambda i: (i, 0))
    piece = pl.BlockSpec((part, step), lambda i: (0, i))
    return pl.pallas_call(
        finish_kernel,
        grid=(rows // step,),
        in_specs=[
            pl.BlockSpec(memory_space=pltpu.SMEM),
            piece,
            piece,
            piece,
            piece,
            whole(w.shape),
            row_block,
            row_block,
            row_block,
        ],
        out_specs=row_block,
        out_shape=jax.ShapeDtypeStruct((rows, width), BF),
        compiler_params=params(),
        cost_estimate=cost(2 * rows * 4 * part * width, rows * width * 16),
        name="finish",
    )(col, *mixed, w, g0, g1, trans)


def swap(x, bit):
    return lax.ppermute(x, "grp", [(i, i ^ bit) for i in range(4)])


def body(
    act,
    cond,
    pair,
    pair_gain,
    chain_ids,
    bias_proj,
    chain_bias,
    cond_gain,
    ada_scale,
    ada_shift,
    qkvg,
    attn_out,
    out_gate,
    trans_in,
    trans_out,
):
    samples, rows, width = act.shape
    flat = samples * rows
    part = qkvg.shape[2]
    heads = part // HD
    col = lax.axis_index("col")
    row = lax.axis_index("row")
    grp = lax.axis_index("grp")
    act = act.reshape(flat, width)
    cond = cond.reshape(flat, cond.shape[2])
    tiles = tile_bias(pair, pair_gain, bias_proj)
    tiles = tiles.reshape(4, heads, *tiles.shape[1:])
    tiles = lax.all_to_all(tiles, "col", 0, 0, tiled=True)
    bias0 = lax.all_to_all(spread_bias(tiles, 16), "row", 0, 0, tiled=True)
    w_proj = jnp.transpose(qkvg, (1, 2, 0))
    qkv, gates, cond_norm = project(act, cond, cond_gain, ada_scale, ada_shift, w_proj)
    qkv = lax.all_to_all(qkv.reshape(16, 3 * HD, 128), "row", 0, 0, tiled=True)
    bias2 = swap(bias0, 2)
    bias1 = swap(bias0, 1)
    bias3 = swap(bias2, 1)
    w_out_full = lax.all_gather(attn_out, "col", axis=0, tiled=True)
    trans_part, g0, g1 = transition(
        act, cond_norm, ada_scale, ada_shift, out_gate, trans_in.reshape(width, -1), trans_out
    )
    trans_total = lax.psum(trans_part, "col")
    head = col * heads + row // 4
    chain = lax.dynamic_slice_in_dim(chain_bias, head, 1, 1).reshape(2)
    qid = chain_ids.reshape(-1, 1)
    kid = jnp.transpose(chain_ids.reshape(4, 4, rows), (1, 0, 2)).reshape(4, 1, 4 * rows)
    attended = attention(
        grp.astype(jnp.int32).reshape(1), chain, qkv, (bias0, bias1, bias2, bias3), qid, kid
    )
    attended = lax.all_to_all(attended, "row", 0, 0, tiled=True)
    mixed = mix(gates, attended)
    pieces = [mixed] + [
        lax.ppermute(mixed, "col", [((i + k) % 4, i) for i in range(4)]) for k in (1, 2, 3)
    ]
    updated = finish(
        col.astype(jnp.int32).reshape(1),
        pieces,
        w_out_full.reshape(4, part, width),
        g0,
        g1,
        trans_total,
    )
    return updated.reshape(samples, rows, width)


def solution(mesh):
    in_specs = (
        P("grp", "row", None),
        P("grp", "row", None),
        P("row", ("col", "grp"), None),
        P(),
        P(),
        P(),
        P(),
        P(),
        P(),
        P(),
        P(None, None, "col"),
        P("col", None),
        P(),
        P(None, None, "col"),
        P("col", None),
    )
    out_specs = P("grp", "row", None)
    return jax.shard_map(body, mesh=mesh, in_specs=in_specs, out_specs=out_specs, check_vma=False)
```

```python
import jax
import jax.numpy as jnp
from jax import lax
from jax.experimental import pallas as pl
from jax.experimental.pallas import tpu as pltpu
from jax.sharding import PartitionSpec as P

HD = 48
BF = jnp.bfloat16
F32 = jnp.float32
NT = (((1,), (1,)), ((), ()))
TN = (((0,), (0,)), ((), ()))


def dot(left, right, dims=(((1,), (0,)), ((), ()))):
    return lax.dot_general(left, right, dims, preferred_element_type=F32)


def norm_last(values_in):
    center = values_in - jnp.mean(values_in, axis=-1, keepdims=True)
    spread = jnp.mean(center * center, axis=-1, keepdims=True)
    return center * lax.rsqrt(spread + 1e-05)


def params(mib=60):
    return pltpu.CompilerParams(vmem_limit_bytes=mib * 1024 * 1024)


def cost(flops, moved, exps=0):
    return pl.CostEstimate(flops=flops, bytes_accessed=moved, transcendentals=exps)


def whole(shape):
    zeros = (0,) * len(shape)
    return pl.BlockSpec(shape, lambda *_: zeros)


def tile_bias_kernel(pair_ref, gain_ref, proj_ref, o0, o1, o2, o3):
    half, pairs, keys, width = pair_ref.shape
    cols, heads, _ = proj_ref.shape
    mine = lax.axis_index("col")
    rows = jnp.swapaxes(pair_ref[...].astype(F32), 0, 1).reshape(half * pairs * keys, width)
    normed = (norm_last(rows) * gain_ref[...]).astype(BF)
    turned = jnp.concatenate(
        [proj_ref[lax.rem(mine + k, cols)].astype(F32) for k in range(cols)], axis=0
    ).astype(BF)
    found = dot(turned, normed, NT)
    lanes = half * keys
    slabs = [found[:, p * lanes : (p + 1) * lanes][:, None, :] for p in range(pairs)]
    tiles = jnp.concatenate(slabs, axis=1).astype(BF)
    for k, ref in enumerate((o0, o1, o2, o3)):
        ref[...] = tiles[k * heads : (k + 1) * heads]


def tile_bias(pair, gain, proj):
    queries, keys, width = pair.shape
    cols, heads, _ = proj.shape
    split = pair.reshape(2, queries // 2, keys, width)
    step = 16
    return pl.pallas_call(
        tile_bias_kernel,
        grid=(queries // 2 // step,),
        in_specs=[
            pl.BlockSpec((2, step, keys, width), lambda i: (0, i, 0, 0)),
            whole((1, width)),
            whole(proj.shape),
        ],
        out_specs=[pl.BlockSpec((heads, step, 2 * keys), lambda i: (0, i, 0))] * cols,
        out_shape=[jax.ShapeDtypeStruct((heads, queries // 2, 2 * keys), BF)] * cols,
        compiler_params=params(),
        cost_estimate=cost(0, 500_000),
        name="tile_bias",
    )(split, gain.reshape(1, width), proj)


def spread_bias_kernel(t0, t1, t2, t3, out_ref):
    heads, pairs, lanes = t0.shape
    keys = lanes // 2
    copies = out_ref.shape[0] // heads
    for head in range(heads):
        parts = [t[head] for t in (t0, t1, t2, t3)]
        low = jnp.concatenate([p[:, :keys] for p in parts], axis=1)
        high = jnp.concatenate([p[:, keys:] for p in parts], axis=1)
        for copy in range(copies):
            out_ref[head * copies + copy, :pairs] = low
            out_ref[head * copies + copy, pairs:] = high


def spread_bias(tiles, dests):
    heads, pairs, lanes = tiles[0].shape
    shape = (dests, 2 * pairs, 2 * lanes)
    return pl.pallas_call(
        spread_bias_kernel,
        in_specs=[whole(t.shape) for t in tiles],
        out_specs=whole(shape),
        grid=(1,),
        out_shape=jax.ShapeDtypeStruct(shape, BF),
        compiler_params=params(),
        cost_estimate=cost(0, 500_000),
        name="spread_bias",
    )(*tiles)


def project_kernel(act_ref, cond_ref, gain_ref, scale_ref, shift_ref, w_ref, qkv_ref, gate_ref, cn_ref):
    heads, pairs, _, lanes = qkv_ref.shape
    gain = jnp.concatenate([gain_ref[i : i + 1] for i in range(gain_ref.shape[0])], axis=1)
    cond_norm = (norm_last(cond_ref[...].astype(F32)) * gain).astype(BF)
    cn_ref[...] = cond_norm
    act_norm = norm_last(act_ref[...].astype(F32))
    att = (
        jax.nn.sigmoid(dot(cond_norm, scale_ref[0])) * act_norm + dot(cond_norm, shift_ref[0])
    ).astype(BF)
    part = heads * HD
    for which in range(3):
        result = dot(w_ref[which], att, NT).astype(BF)
        for head in range(heads):
            for p in range(pairs):
                qkv_ref[head, p, which * HD : (which + 1) * HD, :] = result[
                    head * HD : (head + 1) * HD, p * lanes : (p + 1) * lanes
                ]
    gate_ref[...] = jax.nn.sigmoid(dot(w_ref[3], att, NT))


def project(act, cond, gain, scale, shift, w):
    rows, width = act.shape
    cwidth = cond.shape[1]
    part = w.shape[1]
    heads = part // HD
    step = 256
    lanes = step
    pairs = rows // lanes
    return pl.pallas_call(
        project_kernel,
        grid=(rows // step,),
        in_specs=[
            pl.BlockSpec((step, width), lambda i: (i, 0)),
            pl.BlockSpec((step, cwidth), lambda i: (i, 0)),
            whole((cwidth // 128, 128)),
            whole((1, cwidth, width)),
            whole((1, cwidth, width)),
            whole(w.shape),
        ],
        out_specs=[
            pl.BlockSpec((heads, 1, 3 * HD, lanes), lambda i: (0, i, 0, 0)),
            pl.BlockSpec((part, step), lambda i: (0, i)),
            pl.BlockSpec((step, cwidth), lambda i: (i, 0)),
        ],
        out_shape=[
            jax.ShapeDtypeStruct((heads, pairs, 3 * HD, lanes), BF),
            jax.ShapeDtypeStruct((part, rows), F32),
            jax.ShapeDtypeStruct((rows, cwidth), BF),
        ],
        compiler_params=params(),
        cost_estimate=cost(
            2 * rows * width * (2 * cwidth + 4 * part), 4 * cwidth * width + 8 * width * part
        ),
        name="project",
    )(act, cond, gain.reshape(cwidth // 128, 128), scale, shift, w)


def transition_kernel(
    act_ref, cn_ref, scale_ref, shift_ref, og_ref, win_ref, wout_ref, last_ref,
    p0, p1, p2, p3, g0_ref, g1_ref, part_ref,
):
    mine = lax.axis_index("col")
    cond_norm = cn_ref[...]
    act_norm = norm_last(act_ref[...].astype(F32))
    tin = (
        jax.nn.sigmoid(dot(cond_norm, scale_ref[0])) * act_norm + dot(cond_norm, shift_ref[0])
    ).astype(BF)
    inner = dot(tin, win_ref[...])
    units = wout_ref.shape[0]
    first = inner[:, :units]
    hidden = (first * jax.nn.sigmoid(first) * inner[:, units:]).astype(BF)
    part_ref[...] = dot(hidden, wout_ref[...]).astype(BF)
    quarter = p0.shape[0]
    for shift, ref in enumerate((p0, p1, p2, p3)):
        start = pl.multiple_of(lax.rem(mine + shift, 4) * quarter, quarter)
        ref[:quarter] = part_ref[pl.ds(start, quarter), :]
        if shift:
            ref[quarter:] = last_ref[...]
    g0_ref[...] = jax.nn.sigmoid(dot(cond_norm, og_ref[0]))
    own = cn_ref[pl.ds(pl.multiple_of(mine * quarter, quarter), quarter), :]
    g1_ref[...] = jax.nn.sigmoid(dot(own, og_ref[1]))


def transition(act, cond_norm, scale, shift, out_gate, w_in, w_out, last):
    rows, width = act.shape
    cwidth = cond_norm.shape[1]
    quarter = rows // 4
    second = pl.BlockSpec((1, cwidth, width), lambda i: (1, 0, 0))
    both = (quarter + last.shape[0], width)
    return pl.pallas_call(
        transition_kernel,
        grid=(1,),
        in_specs=[
            whole(act.shape),
            whole(cond_norm.shape),
            second,
            second,
            whole(out_gate.shape),
            whole(w_in.shape),
            whole(w_out.shape),
            whole(last.shape),
        ],
        out_specs=[whole((quarter, width))]
        + [whole(both)] * 3
        + [whole((rows, width)), whole((quarter, width))],
        out_shape=[jax.ShapeDtypeStruct((quarter, width), BF)]
        + [jax.ShapeDtypeStruct(both, BF)] * 3
        + [
            jax.ShapeDtypeStruct((rows, width), F32),
            jax.ShapeDtypeStruct((quarter, width), F32),
        ],
        scratch_shapes=[pltpu.VMEM((rows, width), BF)],
        compiler_params=params(),
        cost_estimate=cost(0, 2_000_000),
        name="transition",
    )(act, cond_norm, scale, shift, out_gate, w_in, w_out, last)


def gated_sum_kernel(a, b, c, d, gate_ref, out_ref):
    rows = slice(0, a.shape[0])
    total = (a[...].astype(F32) + b[rows].astype(F32)) + (c[rows].astype(F32) + d[rows].astype(F32))
    out_ref[...] = (total * gate_ref[...]).astype(BF)


def gated_sum(parts, gate):
    shape = gate.shape
    return pl.pallas_call(
        gated_sum_kernel,
        grid=(1,),
        in_specs=[whole(shape)] * 5,
        out_specs=whole(shape),
        out_shape=jax.ShapeDtypeStruct(shape, BF),
        compiler_params=params(),
        cost_estimate=cost(4 * gate.size, gate.size * 14),
        name="gated_sum",
    )(*parts, gate)


def attention_kernel(
    chain_ref, own_ref, far_ref, b0, b1, b2, b3, id_ref, out_ref, k_ref, v_ref, kid_ref, turn_ref, qid_ref
):
    samples, pieces, _, span = k_ref.shape
    half = own_ref.shape[2] // samples
    cols = span // half
    blocks = b0.shape[0]
    z, xh, col = (lax.axis_index(name) for name in ("z", "xh", "col"))
    grp = 2 * lax.axis_index("xlo") + lax.axis_index("core")

    @pl.when(pl.program_id(0) == 0)
    def _():
        for piece in range(pieces):
            g = grp ^ piece
            near = (g & 1) == xh
            keys, values, ids = [], [], []
            for k in range(cols):
                token = 4 * lax.rem(col + cols - k, cols) + g
                at = token >> 1
                keys.append(jnp.where(near, own_ref[at, HD : 2 * HD], far_ref[at, :HD]))
                values.append(jnp.where(near, own_ref[at, 2 * HD :], far_ref[at, HD:]))
                line = id_ref[pl.ds(at, 1), :]
                ids.append(jnp.where((g & 1) == 0, line[:, :half], line[:, half:]))
            kid_ref[piece] = jnp.concatenate(ids, axis=1)
            for s in range(samples):
                lanes = slice(s * half, (s + 1) * half)
                k_ref[s, piece] = jnp.concatenate([x[:, lanes] for x in keys], axis=1)
                v_ref[s, piece] = jnp.concatenate([x[:, lanes] for x in values], axis=1)
        turn_ref[...] = jnp.transpose(id_ref[...])
        for at in range(id_ref.shape[0]):
            qid_ref[at] = turn_ref[pl.ds(pl.multiple_of(xh * half, half), half), at : at + 1]

    step = pl.program_id(0)
    head = col * 4 + z // 2
    other, same = chain_ref[0, head], chain_ref[1, head]
    qid = qid_ref[pl.ds(step * blocks, blocks)].reshape(blocks * half, 1)
    totals = []
    for piece, ref in enumerate((b0, b1, b2, b3)):
        bias = ref[...].reshape(blocks * half, span).astype(F32)
        totals.append(bias + jnp.where(qid == kid_ref[piece], same, other))
    scale = HD ** (-0.5)
    results = []
    queries = [own_ref[step * blocks + b, :HD] for b in range(blocks)]
    for s in range(samples):
        lanes = slice(s * half, (s + 1) * half)
        query = jnp.concatenate([q[:, lanes] for q in queries], axis=1)
        scores = [
            lax.dot_general(query, k_ref[s, p], TN, preferred_element_type=F32) * scale + totals[p]
            for p in range(pieces)
        ]
        top = jnp.max(
            jnp.maximum(jnp.maximum(scores[0], scores[1]), jnp.maximum(scores[2], scores[3])),
            axis=1,
            keepdims=True,
        )
        weights = [jnp.exp(x - top) for x in scores]
        total = jnp.sum(
            (weights[0] + weights[1]) + (weights[2] + weights[3]), axis=1, keepdims=True
        )
        summed = sum(dot(weights[p].astype(BF), v_ref[s, p], NT) for p in range(pieces))
        results.append(jnp.transpose(summed / total).astype(BF))
    for b in range(blocks):
        out_ref[b] = jnp.concatenate([r[:, b * half : (b + 1) * half] for r in results], axis=1)


def attention(chain_bias, own, far, biases, ids):
    count, rows, lanes = own.shape
    half = 64
    samples = lanes // half
    span = biases[0].shape[2]
    blocks = 2
    bias_spec = pl.BlockSpec((blocks, half, span), lambda i: (i, 0, 0))
    tokens = 2 * count * half
    return pl.pallas_call(
        attention_kernel,
        grid=(count // blocks,),
        in_specs=[
            pl.BlockSpec(memory_space=pltpu.SMEM),
            whole(own.shape),
            whole(far.shape),
            bias_spec,
            bias_spec,
            bias_spec,
            bias_spec,
            whole(ids.shape),
        ],
        out_specs=pl.BlockSpec((blocks, HD, lanes), lambda i: (i, 0, 0)),
        out_shape=jax.ShapeDtypeStruct((count, HD, lanes), BF),
        scratch_shapes=[
            pltpu.VMEM((samples, 4, HD, span), BF),
            pltpu.VMEM((samples, 4, HD, span), BF),
            pltpu.VMEM((4, 1, span), jnp.int32),
            pltpu.VMEM((ids.shape[1], ids.shape[0]), jnp.int32),
            pltpu.VMEM((count, half, 1), jnp.int32),
        ],
        compiler_params=params(),
        cost_estimate=cost(8 * tokens * tokens * HD, 20_000_000, 2 * tokens * tokens),
        name="attention",
    )(chain_bias, own, far, *biases, ids)


def mix_kernel(gate_ref, o_ref, out_ref):
    dests, _, lanes = o_ref.shape
    pairs = out_ref.shape[1] // lanes
    for r in range(dests):
        rows = slice(r // pairs * HD, (r // pairs + 1) * HD)
        cols = slice(r % pairs * lanes, (r % pairs + 1) * lanes)
        out_ref[rows, cols] = (gate_ref[rows, cols] * o_ref[r].astype(F32)).astype(BF)


def mix(gates, attended):
    return pl.pallas_call(
        mix_kernel,
        grid=(1,),
        in_specs=[whole(gates.shape), whole(attended.shape)],
        out_specs=whole(gates.shape),
        out_shape=jax.ShapeDtypeStruct(gates.shape, BF),
        compiler_params=params(),
        cost_estimate=cost(gates.size, gates.size * 8),
        name="mix",
    )(gates, attended)


def finish_kernel(m0, m1, m2, m3, w0, w1, w2, w3, g0_ref, t0, t1, t2, t3, out_ref, total_ref):
    mine = lax.axis_index("col")
    total = None
    depth = m0.shape[0]
    for ref, w in zip((m0, m1, m2, m3), (w0, w1, w2, w3)):
        term = lax.dot_general(ref[...], w[-depth:], TN, preferred_element_type=F32)
        total = term if total is None else total + term
    total_ref[...] = g0_ref[...] * total
    quarter = t0.shape[0]
    for shift, ref in enumerate((t0, t1, t2, t3)):
        rows = pl.ds(pl.multiple_of(((mine + shift) % 4) * quarter, quarter), quarter)
        out_ref[rows, :] = (total_ref[rows, :] + ref[...].astype(F32)).astype(BF)


def finish(mixed, w, g0, trans):
    rows, width = g0.shape
    return pl.pallas_call(
        finish_kernel,
        grid=(1,),
        in_specs=[whole(x.shape) for x in (*mixed, *w, g0, *trans)],
        out_specs=whole((rows, width)),
        out_shape=jax.ShapeDtypeStruct((rows, width), BF),
        scratch_shapes=[pltpu.VMEM((rows, width), F32)],
        compiler_params=params(),
        cost_estimate=cost(2 * rows * width * width, rows * width * 12),
        name="finish",
    )(*mixed, *w, g0, *trans)


def around(x):
    return [x] + [
        lax.ppermute(x, "col", [((i + k) % 4, i) for i in range(4)]) for k in (1, 3, 2)
    ]


def in_order(pieces):
    return [pieces[0], pieces[1], pieces[3], pieces[2]]


def swap(x, axis):
    return lax.ppermute(x, axis, [(0, 1), (1, 0)])


def send(x, k):
    return lax.ppermute(x, "col", [(i, (i + k) % 4) for i in range(4)])


def around(x):
    return [x, send(x, 3), send(x, 2), send(x, 1)]


def scatter(parts):
    return [parts[0], send(parts[1], 1), send(parts[2], 2), send(parts[3], 3)]


def tie(first, *later):
    return lax.optimization_barrier((first, *later))


def body(
    act,
    cond,
    pair,
    pair_gain,
    chain_ids,
    bias_proj,
    chain_bias,
    cond_gain,
    ada_scale,
    ada_shift,
    qkvg,
    attn_out,
    out_gate,
    trans_in,
    trans_out,
):
    samples, rows, width = act.shape
    flat = samples * rows
    part = qkvg.shape[2]
    heads = part // HD
    act = act.reshape(flat, width)
    cond = cond.reshape(flat, cond.shape[2])
    w_proj = jnp.transpose(qkvg, (1, 2, 0))
    qkv, gates, cond_norm = project(act, cond, cond_gain, ada_scale, ada_shift, w_proj)
    qkv, pair = tie(qkv, pair)
    own = lax.all_to_all(qkv.reshape(8, 3 * HD, 4 * rows), "z", 0, 0, tiled=True)
    proj = jnp.transpose(bias_proj).reshape(4, heads, -1)
    tiles = tile_bias(pair, pair_gain, proj)
    *tiles, act = tie(*tiles, act)
    *parts, g0, g1 = transition(
        act,
        cond_norm,
        ada_scale,
        ada_shift,
        out_gate,
        trans_in.reshape(width, -1),
        trans_out,
        attn_out,
    )
    parts = scatter(parts)
    spread = spread_bias(scatter(tiles), 8)
    own, spread, g0 = tie(own, spread, g0)
    bias0 = lax.all_to_all(spread, "z", 0, 0, tiled=True)
    far = swap(own[:, HD:], "xh")
    bias2 = swap(bias0, "xlo")
    bias1 = swap(bias0, "core")
    bias3 = swap(bias2, "core")
    quarter = gated_sum(parts, g1)
    trans = around(quarter)
    attended = attention(
        chain_bias, own, far, (bias0, bias1, bias2, bias3), chain_ids.reshape(8, 2 * rows)
    )
    attended = lax.all_to_all(attended, "z", 0, 0, tiled=True)
    w_out_all = [attn_out, parts[3], parts[2], parts[1]]
    updated = finish(around(mix(gates, attended)), w_out_all, g0, trans)
    return updated.reshape(samples, rows, width)


def solution(mesh):
    fine = jax.sharding.Mesh(
        mesh.devices.reshape(8, 2, 4, 2, 2), ("z", "xh", "col", "xlo", "core")
    )
    rows, groups = ("z", "xh"), ("xlo", "core")
    in_specs = (
        P(groups, rows, None),
        P(groups, rows, None),
        P(rows, ("col", *groups), None),
        P(),
        P(),
        P(),
        P(),
        P(),
        P(),
        P(),
        P(None, None, "col"),
        P("col", None),
        P(),
        P(None, None, "col"),
        P("col", None),
    )
    out_specs = P(groups, rows, None)
    return jax.shard_map(body, mesh=fine, in_specs=in_specs, out_specs=out_specs, check_vma=False)
```

```python
import jax
import jax.numpy as jnp
from jax import lax
from jax.experimental import pallas as pl
from jax.experimental.pallas import tpu as pltpu
from jax.sharding import PartitionSpec as P

HD = 48
BF = jnp.bfloat16
F32 = jnp.float32
LOG2E = 1.4426950408889634
NT = (((1,), (1,)), ((), ()))
TN = (((0,), (0,)), ((), ()))


def dot(left, right, dims=(((1,), (0,)), ((), ()))):
    return lax.dot_general(left, right, dims, preferred_element_type=F32)


def norm_last(values_in):
    center = values_in - jnp.mean(values_in, axis=-1, keepdims=True)
    spread = jnp.mean(center * center, axis=-1, keepdims=True)
    return center * lax.rsqrt(spread + 1e-05)


def params(mib=60):
    return pltpu.CompilerParams(vmem_limit_bytes=mib * 1024 * 1024)


def cost(flops, moved, exps=0):
    return pl.CostEstimate(flops=flops, bytes_accessed=moved, transcendentals=exps)


def whole(shape):
    zeros = (0,) * len(shape)
    return pl.BlockSpec(shape, lambda *_: zeros)


ANY = pl.BlockSpec(memory_space=pl.ANY)


def fetch(pairs, sems):
    copies = [
        pltpu.make_async_copy(source, target, sems.at[i])
        for i, (source, target) in enumerate(pairs)
    ]
    for copy in copies:
        copy.start()
    return copies


def room(*shapes, dtype=BF):
    return [pltpu.VMEM(shape, dtype) for shape in shapes]


def tile_bias_kernel(pair_ref, gain_ref, proj_ref, o0, o1, o2, o3):
    half, pairs, keys, width = pair_ref.shape
    cols, heads, _ = proj_ref.shape
    mine = lax.axis_index("col")
    rows = jnp.swapaxes(pair_ref[...].astype(F32), 0, 1).reshape(half * pairs * keys, width)
    normed = (norm_last(rows) * gain_ref[...]).astype(BF)
    turned = jnp.concatenate(
        [proj_ref[lax.rem(mine + k, cols)].astype(F32) for k in range(cols)], axis=0
    ).astype(BF)
    found = dot(turned, normed, NT)
    lanes = half * keys
    slabs = [found[:, p * lanes : (p + 1) * lanes][:, None, :] for p in range(pairs)]
    tiles = jnp.concatenate(slabs, axis=1).astype(BF)
    for k, ref in enumerate((o0, o1, o2, o3)):
        ref[...] = tiles[k * heads : (k + 1) * heads]


def tile_bias(pair, gain, proj):
    queries, keys, width = pair.shape
    cols, heads, _ = proj.shape
    split = pair.reshape(2, queries // 2, keys, width)
    step = 16
    return pl.pallas_call(
        tile_bias_kernel,
        grid=(queries // 2 // step,),
        in_specs=[
            pl.BlockSpec((2, step, keys, width), lambda i: (0, i, 0, 0)),
            whole((1, width)),
            whole(proj.shape),
        ],
        out_specs=[pl.BlockSpec((heads, step, 2 * keys), lambda i: (0, i, 0))] * cols,
        out_shape=[jax.ShapeDtypeStruct((heads, queries // 2, 2 * keys), BF)] * cols,
        compiler_params=params(),
        cost_estimate=cost(0, 500_000),
        name="tile_bias",
    )(split, gain.reshape(1, width), proj)


def spread_bias_kernel(t0, t1, t2, t3, out_ref):
    heads, pairs, lanes = t0.shape
    keys = lanes // 2
    copies = out_ref.shape[0] // heads
    for head in range(heads):
        parts = [t[head] for t in (t0, t1, t2, t3)]
        low = jnp.concatenate([p[:, :keys] for p in parts], axis=1)
        high = jnp.concatenate([p[:, keys:] for p in parts], axis=1)
        for copy in range(copies):
            out_ref[head * copies + copy, :pairs] = low
            out_ref[head * copies + copy, pairs:] = high


def spread_bias(tiles, dests):
    heads, pairs, lanes = tiles[0].shape
    shape = (dests, 2 * pairs, 2 * lanes)
    return pl.pallas_call(
        spread_bias_kernel,
        in_specs=[whole(t.shape) for t in tiles],
        out_specs=whole(shape),
        grid=(1,),
        out_shape=jax.ShapeDtypeStruct(shape, BF),
        compiler_params=params(8),
        cost_estimate=cost(0, 500_000),
        name="spread_bias",
    )(*tiles)


def project_kernel(act_ref, cond_ref, gain_ref, scale_ref, shift_ref, w_ref, qkv_ref, gate_ref, cn_ref):
    heads, pairs, _, lanes = qkv_ref.shape
    gain = jnp.concatenate([gain_ref[i : i + 1] for i in range(gain_ref.shape[0])], axis=1)
    cond_norm = (norm_last(cond_ref[...].astype(F32)) * gain).astype(BF)
    cn_ref[...] = cond_norm
    act_norm = norm_last(act_ref[...].astype(F32))
    att = (
        jax.nn.sigmoid(dot(cond_norm, scale_ref[0])) * act_norm + dot(cond_norm, shift_ref[0])
    ).astype(BF)
    part = heads * HD
    for which in range(3):
        result = dot(w_ref[which], att, NT).astype(BF)
        for head in range(heads):
            for p in range(pairs):
                qkv_ref[head, p, which * HD : (which + 1) * HD, :] = result[
                    head * HD : (head + 1) * HD, p * lanes : (p + 1) * lanes
                ]
    gate_ref[...] = jax.nn.sigmoid(dot(w_ref[3], att, NT))


def project(act, cond, gain, scale, shift, w):
    rows, width = act.shape
    cwidth = cond.shape[1]
    part = w.shape[1]
    heads = part // HD
    step = 256
    lanes = step
    pairs = rows // lanes
    return pl.pallas_call(
        project_kernel,
        grid=(rows // step,),
        in_specs=[
            pl.BlockSpec((step, width), lambda i: (i, 0)),
            pl.BlockSpec((step, cwidth), lambda i: (i, 0)),
            whole((cwidth // 128, 128)),
            whole((1, cwidth, width)),
            whole((1, cwidth, width)),
            whole(w.shape),
        ],
        out_specs=[
            pl.BlockSpec((heads, 1, 3 * HD, lanes), lambda i: (0, i, 0, 0)),
            pl.BlockSpec((part, step), lambda i: (0, i)),
            pl.BlockSpec((step, cwidth), lambda i: (i, 0)),
        ],
        out_shape=[
            jax.ShapeDtypeStruct((heads, pairs, 3 * HD, lanes), BF),
            jax.ShapeDtypeStruct((part, rows), F32),
            jax.ShapeDtypeStruct((rows, cwidth), BF),
        ],
        compiler_params=params(),
        cost_estimate=cost(
            2 * rows * width * (2 * cwidth + 4 * part), 4 * cwidth * width + 8 * width * part
        ),
        name="project",
    )(act, cond, gain.reshape(cwidth // 128, 128), scale, shift, w)


def half_rows(rows, other=0):
    start = (lax.axis_index("core") ^ other) * (rows // 2)
    return pl.ds(pl.multiple_of(start, rows // 2), rows // 2)


def transition_kernel(
    act_ref, cn_ref, scale_ref, shift_ref, og_ref, win_ref, wout_ref, last_ref,
    p0, p1, p2, p3, g0_ref, g1_ref, part_ref,
):
    mine = lax.axis_index("col")
    cond_norm = cn_ref[...]
    act_norm = norm_last(act_ref[...].astype(F32))
    tin = (
        jax.nn.sigmoid(dot(cond_norm, scale_ref[0])) * act_norm + dot(cond_norm, shift_ref[0])
    ).astype(BF)
    inner = dot(tin, win_ref[...])
    units = wout_ref.shape[0]
    first = inner[:, :units]
    hidden = (first * jax.nn.sigmoid(first) * inner[:, units:]).astype(BF)
    part_ref[...] = dot(hidden, wout_ref[...]).astype(BF)
    quarter = p0.shape[0]
    for shift, ref in enumerate((p0, p1, p2, p3)):
        start = pl.multiple_of(lax.rem(mine + shift, 4) * quarter, quarter)
        ref[:quarter] = part_ref[pl.ds(start, quarter), :]
        if shift:
            ref[quarter:] = last_ref[half_rows(last_ref.shape[0]), :]
    g0_ref[...] = jax.nn.sigmoid(dot(cond_norm, og_ref[0]))
    own = cn_ref[pl.ds(pl.multiple_of(mine * quarter, quarter), quarter), :]
    g1_ref[...] = jax.nn.sigmoid(dot(own, og_ref[1]))


def transition(act, cond_norm, scale, shift, out_gate, w_in, w_out, last):
    rows, width = act.shape
    cwidth = cond_norm.shape[1]
    quarter = rows // 4
    second = pl.BlockSpec((1, cwidth, width), lambda i: (1, 0, 0))
    both = (quarter + last.shape[0] // 2, width)
    return pl.pallas_call(
        transition_kernel,
        grid=(1,),
        in_specs=[
            whole(act.shape),
            whole(cond_norm.shape),
            second,
            second,
            whole(out_gate.shape),
            whole(w_in.shape),
            whole(w_out.shape),
            whole(last.shape),
        ],
        out_specs=[whole((quarter, width))]
        + [whole(both)] * 3
        + [whole((rows, width)), whole((quarter, width))],
        out_shape=[jax.ShapeDtypeStruct((quarter, width), BF)]
        + [jax.ShapeDtypeStruct(both, BF)] * 3
        + [
            jax.ShapeDtypeStruct((rows, width), F32),
            jax.ShapeDtypeStruct((quarter, width), F32),
        ],
        scratch_shapes=[pltpu.VMEM((rows, width), BF)],
        compiler_params=params(),
        cost_estimate=cost(0, 2_000_000),
        name="transition",
    )(act, cond_norm, scale, shift, out_gate, w_in, w_out, last)


def gated_sum_kernel(a, b, c, d, gate_ref, out_ref, pack_ref):
    rows = slice(0, a.shape[0])
    total = (a[...].astype(F32) + b[rows].astype(F32)) + (c[rows].astype(F32) + d[rows].astype(F32))
    out_ref[...] = (total * gate_ref[...]).astype(BF)
    for i, ref in enumerate((d, c, b)):
        pack_ref[i] = ref[a.shape[0] :]


def gated_sum(parts, gate):
    shape = gate.shape
    pack = (3, parts[1].shape[0] - shape[0], shape[1])
    return pl.pallas_call(
        gated_sum_kernel,
        grid=(1,),
        in_specs=[whole(x.shape) for x in (*parts, gate)],
        out_specs=[whole(shape), whole(pack)],
        out_shape=[jax.ShapeDtypeStruct(shape, BF), jax.ShapeDtypeStruct(pack, BF)],
        compiler_params=params(8),
        cost_estimate=cost(30_000_000_000, 1000),
        name="gated_sum",
    )(*parts, gate)


def attention_kernel(
    chain_ref, own_ref, far_ref, b0, b1, b2, b3, id_ref, out_ref, k_ref, v_ref, kid_ref, turn_ref, qid_ref
):
    samples, cols, pieces = k_ref.shape[0], 4, 4
    half = own_ref.shape[2] // samples
    span = cols * half
    blocks = b0.shape[0]
    z, xh, col = (lax.axis_index(name) for name in ("z", "xh", "col"))
    grp = 2 * lax.axis_index("xlo") + lax.axis_index("core")

    @pl.when(pl.program_id(0) == 0)
    def _():
        for piece in range(pieces):
            g = grp ^ piece
            near = (g & 1) == xh
            keys, values, ids = [], [], []
            for k in range(cols):
                token = 4 * lax.rem(col + cols - k, cols) + g
                at = token >> 1
                keys.append(jnp.where(near, own_ref[at, HD : 2 * HD], far_ref[at, :HD]))
                values.append(jnp.where(near, own_ref[at, 2 * HD :], far_ref[at, HD:]))
                line = id_ref[pl.ds(at, 1), :]
                ids.append(jnp.where((g & 1) == 0, line[:, :half], line[:, half:]))
            here = slice(piece * span, (piece + 1) * span)
            kid_ref[:, here] = jnp.concatenate(ids, axis=1)
            for s in range(samples):
                lanes = slice(s * half, (s + 1) * half)
                k_ref[s, :, here] = jnp.concatenate([x[:, lanes] for x in keys], axis=1)
                v_ref[s, :, here] = jnp.concatenate([x[:, lanes] for x in values], axis=1)
        turn_ref[...] = jnp.transpose(id_ref[...])
        for at in range(id_ref.shape[0]):
            qid_ref[at] = turn_ref[pl.ds(pl.multiple_of(xh * half, half), half), at : at + 1]

    step = pl.program_id(0)
    head = col * 4 + z // 2
    other, same = chain_ref[0, head] * LOG2E, chain_ref[1, head] * LOG2E
    qid = qid_ref[pl.ds(step * blocks, blocks)].reshape(blocks * half, 1)
    bias = jnp.concatenate(
        [ref[...].reshape(blocks * half, span) for ref in (b0, b1, b2, b3)], axis=1
    ).astype(F32)
    bias = bias * LOG2E + jnp.where(qid == kid_ref[...], same, other)
    scale = HD ** (-0.5) * LOG2E
    results = []
    queries = [own_ref[step * blocks + b, :HD] for b in range(blocks)]
    for s in range(samples):
        lanes = slice(s * half, (s + 1) * half)
        query = jnp.concatenate([q[:, lanes] for q in queries], axis=1)
        scores = dot(query, k_ref[s], TN) * scale + bias
        weights = jnp.exp2(scores - jnp.max(scores, axis=1, keepdims=True))
        total = jnp.sum(weights, axis=1, keepdims=True)
        summed = dot(weights.astype(BF), v_ref[s], NT)
        results.append(jnp.transpose(summed / total).astype(BF))
    for b in range(blocks):
        out_ref[b] = jnp.concatenate([r[:, b * half : (b + 1) * half] for r in results], axis=1)


def attention(chain_bias, own, far, biases, ids):
    count, rows, lanes = own.shape
    half = 64
    samples = lanes // half
    span = biases[0].shape[2]
    blocks = count
    bias_spec = pl.BlockSpec((blocks, half, span), lambda i: (i, 0, 0))
    tokens = 2 * count * half
    return pl.pallas_call(
        attention_kernel,
        grid=(count // blocks,),
        in_specs=[
            pl.BlockSpec(memory_space=pltpu.SMEM),
            whole(own.shape),
            whole(far.shape),
            bias_spec,
            bias_spec,
            bias_spec,
            bias_spec,
            whole(ids.shape),
        ],
        out_specs=pl.BlockSpec((blocks, HD, lanes), lambda i: (i, 0, 0)),
        out_shape=jax.ShapeDtypeStruct((count, HD, lanes), BF),
        scratch_shapes=[
            pltpu.VMEM((samples, HD, 4 * span), BF),
            pltpu.VMEM((samples, HD, 4 * span), BF),
            pltpu.VMEM((1, 4 * span), jnp.int32),
            pltpu.VMEM((ids.shape[1], ids.shape[0]), jnp.int32),
            pltpu.VMEM((count, half, 1), jnp.int32),
        ],
        compiler_params=params(32),
        cost_estimate=cost(0, 1000),
        name="attention",
    )(chain_bias, own, far, *biases, ids)


def mix_kernel(gate_ref, o_ref, out_ref):
    dests, _, lanes = o_ref.shape
    pairs = out_ref.shape[1] // lanes
    for r in range(dests):
        rows = slice(r // pairs * HD, (r // pairs + 1) * HD)
        cols = slice(r % pairs * lanes, (r % pairs + 1) * lanes)
        out_ref[rows, cols] = (gate_ref[rows, cols] * o_ref[r].astype(F32)).astype(BF)


def mix(gates, attended):
    return pl.pallas_call(
        mix_kernel,
        grid=(1,),
        in_specs=[whole(gates.shape), whole(attended.shape)],
        out_specs=whole(gates.shape),
        out_shape=jax.ShapeDtypeStruct(gates.shape, BF),
        compiler_params=params(8),
        cost_estimate=cost(gates.size, gates.size * 8),
        name="mix",
    )(gates, attended)


def finish_kernel(
    m0, m1, m2, m3, w0, wa, wb, g0_hbm, t0, t1, t2, t3, out_hbm,
    m_ref, w_ref, g0_ref, t_ref, total_ref, out_ref, in_sems, out_sems,
):
    mine = lax.axis_index("col")
    depth = w_ref.shape[1]
    copies = fetch(
        [
            *[(source, m_ref.at[i]) for i, source in enumerate((m0, m1, m2, m3))],
            (w0, w_ref.at[0]),
            *[(wa.at[i], w_ref.at[i + 1, half_rows(depth)]) for i in range(3)],
            *[(wb.at[i], w_ref.at[i + 1, half_rows(depth, 1)]) for i in range(3)],
            (g0_hbm, g0_ref),
            *[(source, t_ref.at[i]) for i, source in enumerate((t0, t1, t2, t3))],
        ],
        in_sems,
    )
    for i in range(11):
        copies[i].wait()
    mixed = m_ref[...].reshape(-1, m_ref.shape[2])
    total = dot(mixed, w_ref[...].reshape(-1, w_ref.shape[2]), TN)
    copies[11].wait()
    total_ref[...] = g0_ref[...] * total
    quarter = t_ref.shape[1]
    outs = []
    for shift in range(4):
        copies[12 + shift].wait()
        rows = pl.ds(pl.multiple_of(lax.rem(mine + shift, 4) * quarter, quarter), quarter)
        out_ref[shift] = (total_ref[rows, :] + t_ref[shift].astype(F32)).astype(BF)
        outs.append(pltpu.make_async_copy(out_ref.at[shift], out_hbm.at[rows], out_sems.at[shift]))
        outs[shift].start()
    for copy in outs:
        copy.wait()


def finish(mixed, w, g0, trans):
    rows, width = g0.shape
    return pl.pallas_call(
        finish_kernel,
        in_specs=[ANY] * 12,
        out_specs=ANY,
        out_shape=jax.ShapeDtypeStruct((rows, width), BF),
        scratch_shapes=[
            pltpu.VMEM((4, *mixed[0].shape), BF),
            pltpu.VMEM((4, *w[0].shape), BF),
            pltpu.VMEM((rows, width), F32),
            pltpu.VMEM((4, rows // 4, width), BF),
            pltpu.VMEM((rows, width), F32),
            pltpu.VMEM((4, rows // 4, width), BF),
            pltpu.SemaphoreType.DMA((16,)),
            pltpu.SemaphoreType.DMA((4,)),
        ],
        compiler_params=params(),
        cost_estimate=cost(2 * rows * width * width, rows * width * 12),
        name="finish",
    )(*mixed, *w, g0, *trans)


def swap(x, axis):
    return lax.ppermute(x, axis, [(0, 1), (1, 0)])


def send(x, k):
    return lax.ppermute(x, "col", [(i, (i + k) % 4) for i in range(4)])


def around(x):
    return [x, send(x, 3), send(x, 2), send(x, 1)]


def scatter(parts):
    return [parts[0], send(parts[1], 1), send(parts[2], 2), send(parts[3], 3)]


def tie(first, *later):
    return lax.optimization_barrier((first, *later))


def body(
    act,
    cond,
    pair,
    pair_gain,
    chain_ids,
    bias_proj,
    chain_bias,
    cond_gain,
    ada_scale,
    ada_shift,
    qkvg,
    attn_out,
    out_gate,
    trans_in,
    trans_out,
):
    samples, rows, width = act.shape
    flat = samples * rows
    part = qkvg.shape[2]
    heads = part // HD
    act = act.reshape(flat, width)
    cond = cond.reshape(flat, cond.shape[2])
    w_proj = jnp.transpose(qkvg, (1, 2, 0))
    qkv, gates, cond_norm = project(act, cond, cond_gain, ada_scale, ada_shift, w_proj)
    qkv, pair = tie(qkv, pair)
    own = lax.all_to_all(qkv.reshape(8, 3 * HD, 4 * rows), "z", 0, 0, tiled=True)
    proj = jnp.transpose(bias_proj).reshape(4, heads, -1)
    tiles = tile_bias(pair, pair_gain, proj)
    spread = spread_bias(scatter(tiles), 8)
    win = trans_in.reshape(width, -1)
    own, spread, act, win = tie(own, spread, act, win)
    bias0 = lax.all_to_all(spread, "z", 0, 0, tiled=True)
    far = swap(own[:, HD:], "xh")
    *parts, g0, g1 = transition(
        act, cond_norm, ada_scale, ada_shift, out_gate, win, trans_out, attn_out
    )
    bias0, g0 = tie(bias0, g0)
    far, *parts = tie(far, *parts)
    parts = scatter(parts)
    bias2 = swap(bias0, "xlo")
    bias1 = swap(bias0, "core")
    bias3 = swap(bias2, "core")
    quarter, pack = gated_sum(parts, g1)
    trans = around(quarter)
    w_out_all = [attn_out, pack, swap(pack, "core")]
    attended = attention(
        chain_bias, own, far, (bias0, bias1, bias2, bias3), chain_ids.reshape(8, 2 * rows)
    )
    attended = lax.all_to_all(attended, "z", 0, 0, tiled=True)
    updated = finish(around(mix(gates, attended)), w_out_all, g0, trans)
    return updated.reshape(samples, rows, width)


def solution(mesh):
    fine = jax.sharding.Mesh(
        mesh.devices.reshape(8, 2, 4, 2, 2), ("z", "xh", "col", "xlo", "core")
    )
    rows, groups = ("z", "xh"), ("xlo", "core")
    in_specs = (
        P(groups, rows, None),
        P(groups, rows, None),
        P(rows, ("col", *groups), None),
        P(),
        P(),
        P(),
        P(),
        P(),
        P(),
        P(),
        P(None, None, "col"),
        P("col", None),
        P(),
        P(None, None, "col"),
        P("col", None),
    )
    out_specs = P(groups, rows, None)
    return jax.shard_map(body, mesh=fine, in_specs=in_specs, out_specs=out_specs, check_vma=False)
```

```python
import jax
import jax.numpy as jnp
from jax import lax
from jax.experimental import pallas as pl
from jax.experimental.pallas import tpu as pltpu
from jax.sharding import PartitionSpec as P

HD = 48
BF = jnp.bfloat16
F32 = jnp.float32
LOG2E = 1.4426950408889634
NT = (((1,), (1,)), ((), ()))
TN = (((0,), (0,)), ((), ()))


def dot(left, right, dims=(((1,), (0,)), ((), ()))):
    return lax.dot_general(left, right, dims, preferred_element_type=F32)


def norm_last(values_in):
    center = values_in - jnp.mean(values_in, axis=-1, keepdims=True)
    spread = jnp.mean(center * center, axis=-1, keepdims=True)
    return center * lax.rsqrt(spread + 1e-05)


def params(mib=60):
    return pltpu.CompilerParams(vmem_limit_bytes=mib * 1024 * 1024)


def cost(flops, moved, exps=0):
    return pl.CostEstimate(flops=flops, bytes_accessed=moved, transcendentals=exps)


def whole(shape):
    zeros = (0,) * len(shape)
    return pl.BlockSpec(shape, lambda *_: zeros)


ANY = pl.BlockSpec(memory_space=pl.ANY)


def fetch(pairs, sems):
    copies = [
        pltpu.make_async_copy(source, target, sems.at[i])
        for i, (source, target) in enumerate(pairs)
    ]
    for copy in copies:
        copy.start()
    return copies


def room(*shapes, dtype=BF):
    return [pltpu.VMEM(shape, dtype) for shape in shapes]


def tile_bias_kernel(pair_ref, gain_ref, proj_ref, o0, o1, o2, o3):
    half, pairs, keys, width = pair_ref.shape
    cols, heads, _ = proj_ref.shape
    mine = lax.axis_index("col")
    rows = jnp.swapaxes(pair_ref[...].astype(F32), 0, 1).reshape(half * pairs * keys, width)
    normed = (norm_last(rows) * gain_ref[...]).astype(BF)
    turned = jnp.concatenate(
        [proj_ref[lax.rem(mine + k, cols)].astype(F32) for k in range(cols)], axis=0
    ).astype(BF)
    found = dot(turned, normed, NT)
    lanes = half * keys
    slabs = [found[:, p * lanes : (p + 1) * lanes][:, None, :] for p in range(pairs)]
    tiles = jnp.concatenate(slabs, axis=1).astype(BF)
    for k, ref in enumerate((o0, o1, o2, o3)):
        ref[...] = tiles[k * heads : (k + 1) * heads]


def tile_bias(pair, gain, proj):
    queries, keys, width = pair.shape
    cols, heads, _ = proj.shape
    split = pair.reshape(2, queries // 2, keys, width)
    step = 16
    return pl.pallas_call(
        tile_bias_kernel,
        grid=(queries // 2 // step,),
        in_specs=[
            pl.BlockSpec((2, step, keys, width), lambda i: (0, i, 0, 0)),
            whole((1, width)),
            whole(proj.shape),
        ],
        out_specs=[pl.BlockSpec((heads, step, 2 * keys), lambda i: (0, i, 0))] * cols,
        out_shape=[jax.ShapeDtypeStruct((heads, queries // 2, 2 * keys), BF)] * cols,
        compiler_params=params(),
        cost_estimate=cost(0, 500_000),
        name="tile_bias",
    )(split, gain.reshape(1, width), proj)


def spread_bias_kernel(t0, t1, t2, t3, out_ref):
    heads, pairs, lanes = t0.shape
    keys = lanes // 2
    copies = out_ref.shape[0] // heads
    for head in range(heads):
        parts = [t[head] for t in (t0, t1, t2, t3)]
        low = jnp.concatenate([p[:, :keys] for p in parts], axis=1)
        high = jnp.concatenate([p[:, keys:] for p in parts], axis=1)
        for copy in range(copies):
            out_ref[head * copies + copy, :pairs] = low
            out_ref[head * copies + copy, pairs:] = high


def spread_bias(tiles, dests):
    heads, pairs, lanes = tiles[0].shape
    shape = (dests, 2 * pairs, 2 * lanes)
    return pl.pallas_call(
        spread_bias_kernel,
        in_specs=[whole(t.shape) for t in tiles],
        out_specs=whole(shape),
        grid=(1,),
        out_shape=jax.ShapeDtypeStruct(shape, BF),
        compiler_params=params(8),
        cost_estimate=cost(0, 500_000),
        name="spread_bias",
    )(*tiles)


def project_kernel(act_ref, cond_ref, gain_ref, scale_ref, shift_ref, w_ref, qkv_ref, gate_ref, cn_ref):
    heads, pairs, _, lanes = qkv_ref.shape
    gain = jnp.concatenate([gain_ref[i : i + 1] for i in range(gain_ref.shape[0])], axis=1)
    cond_norm = (norm_last(cond_ref[...].astype(F32)) * gain).astype(BF)
    cn_ref[...] = cond_norm
    act_norm = norm_last(act_ref[...].astype(F32))
    att = (
        jax.nn.sigmoid(dot(cond_norm, scale_ref[0])) * act_norm + dot(cond_norm, shift_ref[0])
    ).astype(BF)
    part = heads * HD
    for which in range(3):
        result = dot(w_ref[which], att, NT).astype(BF)
        for head in range(heads):
            for p in range(pairs):
                qkv_ref[head, p, which * HD : (which + 1) * HD, :] = result[
                    head * HD : (head + 1) * HD, p * lanes : (p + 1) * lanes
                ]
    gate_ref[...] = jax.nn.sigmoid(dot(w_ref[3], att, NT))


def project(act, cond, gain, scale, shift, w):
    rows, width = act.shape
    cwidth = cond.shape[1]
    part = w.shape[1]
    heads = part // HD
    step = 256
    lanes = step
    pairs = rows // lanes
    return pl.pallas_call(
        project_kernel,
        grid=(rows // step,),
        in_specs=[
            pl.BlockSpec((step, width), lambda i: (i, 0)),
            pl.BlockSpec((step, cwidth), lambda i: (i, 0)),
            whole((cwidth // 128, 128)),
            whole((1, cwidth, width)),
            whole((1, cwidth, width)),
            whole(w.shape),
        ],
        out_specs=[
            pl.BlockSpec((heads, 1, 3 * HD, lanes), lambda i: (0, i, 0, 0)),
            pl.BlockSpec((part, step), lambda i: (0, i)),
            pl.BlockSpec((step, cwidth), lambda i: (i, 0)),
        ],
        out_shape=[
            jax.ShapeDtypeStruct((heads, pairs, 3 * HD, lanes), BF),
            jax.ShapeDtypeStruct((part, rows), F32),
            jax.ShapeDtypeStruct((rows, cwidth), BF),
        ],
        compiler_params=params(),
        cost_estimate=cost(
            2 * rows * width * (2 * cwidth + 4 * part), 4 * cwidth * width + 8 * width * part
        ),
        name="project",
    )(act, cond, gain.reshape(cwidth // 128, 128), scale, shift, w)


def half_rows(rows, other=0):
    start = (lax.axis_index("core") ^ other) * (rows // 2)
    return pl.ds(pl.multiple_of(start, rows // 2), rows // 2)


def transition_kernel(
    act_ref, cn_ref, scale_ref, shift_ref, og_ref, win_ref, wout_ref, last_ref,
    p0, p1, p2, p3, g1_ref, part_ref,
):
    mine = lax.axis_index("col")
    cond_norm = cn_ref[...]
    act_norm = norm_last(act_ref[...].astype(F32))
    tin = (
        jax.nn.sigmoid(dot(cond_norm, scale_ref[0])) * act_norm + dot(cond_norm, shift_ref[0])
    ).astype(BF)
    inner = dot(tin, win_ref[...])
    units = wout_ref.shape[0]
    first = inner[:, :units]
    hidden = (first * jax.nn.sigmoid(first) * inner[:, units:]).astype(BF)
    part_ref[...] = dot(hidden, wout_ref[...]).astype(BF)
    quarter = p0.shape[0]
    for shift, ref in enumerate((p0, p1, p2, p3)):
        start = pl.multiple_of(lax.rem(mine + shift, 4) * quarter, quarter)
        ref[:quarter] = part_ref[pl.ds(start, quarter), :]
        if shift:
            ref[quarter:] = last_ref[half_rows(last_ref.shape[0]), :]
    own = cn_ref[pl.ds(pl.multiple_of(mine * quarter, quarter), quarter), :]
    g1_ref[...] = jax.nn.sigmoid(dot(own, og_ref[0]))


def transition(act, cond_norm, scale, shift, out_gate, w_in, w_out, last):
    rows, width = act.shape
    cwidth = cond_norm.shape[1]
    quarter = rows // 4
    second = pl.BlockSpec((1, cwidth, width), lambda i: (1, 0, 0))
    both = (quarter + last.shape[0] // 2, width)
    return pl.pallas_call(
        transition_kernel,
        grid=(1,),
        in_specs=[
            whole(act.shape),
            whole(cond_norm.shape),
            second,
            second,
            second,
            whole(w_in.shape),
            whole(w_out.shape),
            whole(last.shape),
        ],
        out_specs=[whole((quarter, width))]
        + [whole(both)] * 3
        + [whole((quarter, width))],
        out_shape=[jax.ShapeDtypeStruct((quarter, width), BF)]
        + [jax.ShapeDtypeStruct(both, BF)] * 3
        + [
            jax.ShapeDtypeStruct((quarter, width), F32),
        ],
        scratch_shapes=[pltpu.VMEM((rows, width), BF)],
        compiler_params=params(),
        cost_estimate=cost(0, 2_000_000),
        name="transition",
    )(act, cond_norm, scale, shift, out_gate, w_in, w_out, last)


def gated_sum_kernel(a, b, c, d, gate_ref, out_ref, pack_ref):
    rows = slice(0, a.shape[0])
    total = (a[...].astype(F32) + b[rows].astype(F32)) + (c[rows].astype(F32) + d[rows].astype(F32))
    out_ref[...] = (total * gate_ref[...]).astype(BF)
    for i, ref in enumerate((d, c, b)):
        pack_ref[i] = ref[a.shape[0] :]


def gated_sum(parts, gate):
    shape = gate.shape
    pack = (3, parts[1].shape[0] - shape[0], shape[1])
    return pl.pallas_call(
        gated_sum_kernel,
        grid=(1,),
        in_specs=[whole(x.shape) for x in (*parts, gate)],
        out_specs=[whole(shape), whole(pack)],
        out_shape=[jax.ShapeDtypeStruct(shape, BF), jax.ShapeDtypeStruct(pack, BF)],
        compiler_params=params(8),
        cost_estimate=cost(30_000_000_000, 1000),
        name="gated_sum",
    )(*parts, gate)


def attention_kernel(
    chain_ref, own_ref, far_ref, b0, b1, b2, b3, id_ref, out_ref, k_ref, v_ref, kid_ref, turn_ref, qid_ref
):
    samples, cols, pieces = k_ref.shape[0], 4, 4
    half = own_ref.shape[2] // samples
    span = cols * half
    blocks = b0.shape[0]
    z, xh, col = (lax.axis_index(name) for name in ("z", "xh", "col"))
    grp = 2 * lax.axis_index("xlo") + lax.axis_index("core")

    @pl.when(pl.program_id(0) == 0)
    def _():
        for piece in range(pieces):
            g = grp ^ piece
            near = (g & 1) == xh
            keys, values, ids = [], [], []
            for k in range(cols):
                token = 4 * lax.rem(col + cols - k, cols) + g
                at = token >> 1
                keys.append(jnp.where(near, own_ref[at, HD : 2 * HD], far_ref[at, :HD]))
                values.append(jnp.where(near, own_ref[at, 2 * HD :], far_ref[at, HD:]))
                line = id_ref[pl.ds(at, 1), :]
                ids.append(jnp.where((g & 1) == 0, line[:, :half], line[:, half:]))
            here = slice(piece * span, (piece + 1) * span)
            kid_ref[:, here] = jnp.concatenate(ids, axis=1)
            for s in range(samples):
                lanes = slice(s * half, (s + 1) * half)
                k_ref[s, :, here] = jnp.concatenate([x[:, lanes] for x in keys], axis=1)
                v_ref[s, :, here] = jnp.concatenate([x[:, lanes] for x in values], axis=1)
        turn_ref[...] = jnp.transpose(id_ref[...])
        for at in range(id_ref.shape[0]):
            qid_ref[at] = turn_ref[pl.ds(pl.multiple_of(xh * half, half), half), at : at + 1]

    step = pl.program_id(0)
    head = col * 4 + z // 2
    other, same = chain_ref[0, head] * LOG2E, chain_ref[1, head] * LOG2E
    qid = qid_ref[pl.ds(step * blocks, blocks)].reshape(blocks * half, 1)
    bias = jnp.concatenate(
        [ref[...].reshape(blocks * half, span) for ref in (b0, b1, b2, b3)], axis=1
    ).astype(F32)
    bias = bias * LOG2E + jnp.where(qid == kid_ref[...], same, other)
    scale = HD ** (-0.5) * LOG2E
    results = []
    queries = [own_ref[step * blocks + b, :HD] for b in range(blocks)]
    for s in range(samples):
        lanes = slice(s * half, (s + 1) * half)
        query = jnp.concatenate([q[:, lanes] for q in queries], axis=1)
        scores = dot(query, k_ref[s], TN) * scale + bias
        weights = jnp.exp2(scores - jnp.max(scores, axis=1, keepdims=True))
        total = jnp.sum(weights, axis=1, keepdims=True)
        summed = dot(weights.astype(BF), v_ref[s], NT)
        results.append(jnp.transpose(summed / total).astype(BF))
    for b in range(blocks):
        out_ref[b] = jnp.concatenate([r[:, b * half : (b + 1) * half] for r in results], axis=1)


def attention(chain_bias, own, far, biases, ids):
    count, rows, lanes = own.shape
    half = 64
    samples = lanes // half
    span = biases[0].shape[2]
    blocks = count
    bias_spec = pl.BlockSpec((blocks, half, span), lambda i: (i, 0, 0))
    tokens = 2 * count * half
    return pl.pallas_call(
        attention_kernel,
        grid=(count // blocks,),
        in_specs=[
            pl.BlockSpec(memory_space=pltpu.SMEM),
            whole(own.shape),
            whole(far.shape),
            bias_spec,
            bias_spec,
            bias_spec,
            bias_spec,
            whole(ids.shape),
        ],
        out_specs=pl.BlockSpec((blocks, HD, lanes), lambda i: (i, 0, 0)),
        out_shape=jax.ShapeDtypeStruct((count, HD, lanes), BF),
        scratch_shapes=[
            pltpu.VMEM((samples, HD, 4 * span), BF),
            pltpu.VMEM((samples, HD, 4 * span), BF),
            pltpu.VMEM((1, 4 * span), jnp.int32),
            pltpu.VMEM((ids.shape[1], ids.shape[0]), jnp.int32),
            pltpu.VMEM((count, half, 1), jnp.int32),
        ],
        compiler_params=params(32),
        cost_estimate=cost(0, 1000),
        name="attention",
    )(chain_bias, own, far, *biases, ids)


def mix_kernel(gate_ref, o_ref, out_ref):
    dests, _, lanes = o_ref.shape
    pairs = out_ref.shape[1] // lanes
    for r in range(dests):
        rows = slice(r // pairs * HD, (r // pairs + 1) * HD)
        cols = slice(r % pairs * lanes, (r % pairs + 1) * lanes)
        out_ref[rows, cols] = (gate_ref[rows, cols] * o_ref[r].astype(F32)).astype(BF)


def mix(gates, attended):
    return pl.pallas_call(
        mix_kernel,
        grid=(1,),
        in_specs=[whole(gates.shape), whole(attended.shape)],
        out_specs=whole(gates.shape),
        out_shape=jax.ShapeDtypeStruct(gates.shape, BF),
        compiler_params=params(8),
        cost_estimate=cost(gates.size, gates.size * 8),
        name="mix",
    )(gates, attended)


def finish_kernel(
    m0, m1, m2, m3, w0, wa, wb, cn_hbm, og_hbm, t0, t1, t2, t3, out_hbm,
    m_ref, w_ref, cn_ref, og_ref, t_ref, total_ref, out_ref, in_sems, out_sems,
):
    mine = lax.axis_index("col")
    depth = w_ref.shape[1]
    copies = fetch(
        [
            (cn_hbm, cn_ref),
            (og_hbm.at[0], og_ref),
            *[(source, m_ref.at[i]) for i, source in enumerate((m0, m1, m2, m3))],
            (w0, w_ref.at[0]),
            *[(wa.at[i], w_ref.at[i + 1, half_rows(depth)]) for i in range(3)],
            *[(wb.at[i], w_ref.at[i + 1, half_rows(depth, 1)]) for i in range(3)],
            *[(source, t_ref.at[i]) for i, source in enumerate((t0, t1, t2, t3))],
        ],
        in_sems,
    )
    copies[0].wait()
    copies[1].wait()
    total_ref[...] = jax.nn.sigmoid(dot(cn_ref[...], og_ref[...]))
    for i in range(2, 13):
        copies[i].wait()
    mixed = m_ref[...].reshape(-1, m_ref.shape[2])
    total = dot(mixed, w_ref[...].reshape(-1, w_ref.shape[2]), TN)
    total_ref[...] = total_ref[...] * total
    quarter = t_ref.shape[1]
    outs = []
    for shift in range(4):
        copies[13 + shift].wait()
        rows = pl.ds(pl.multiple_of(lax.rem(mine + shift, 4) * quarter, quarter), quarter)
        out_ref[shift] = (total_ref[rows, :] + t_ref[shift].astype(F32)).astype(BF)
        outs.append(pltpu.make_async_copy(out_ref.at[shift], out_hbm.at[rows], out_sems.at[shift]))
        outs[shift].start()
    for copy in outs:
        copy.wait()


def finish(mixed, w, cond_norm, out_gate, trans):
    rows, cwidth = cond_norm.shape
    width = out_gate.shape[2]
    return pl.pallas_call(
        finish_kernel,
        in_specs=[ANY] * 13,
        out_specs=ANY,
        out_shape=jax.ShapeDtypeStruct((rows, width), BF),
        scratch_shapes=[
            pltpu.VMEM((4, *mixed[0].shape), BF),
            pltpu.VMEM((4, *w[0].shape), BF),
            pltpu.VMEM((rows, cwidth), BF),
            pltpu.VMEM((cwidth, width), BF),
            pltpu.VMEM((4, rows // 4, width), BF),
            pltpu.VMEM((rows, width), F32),
            pltpu.VMEM((4, rows // 4, width), BF),
            pltpu.SemaphoreType.DMA((17,)),
            pltpu.SemaphoreType.DMA((4,)),
        ],
        compiler_params=params(),
        cost_estimate=cost(2 * rows * width * width, rows * width * 12),
        name="finish",
    )(*mixed, *w, cond_norm, out_gate, *trans)


def swap(x, axis):
    return lax.ppermute(x, axis, [(0, 1), (1, 0)])


def send(x, k):
    return lax.ppermute(x, "col", [(i, (i + k) % 4) for i in range(4)])


def around(x):
    return [x, send(x, 3), send(x, 2), send(x, 1)]


def scatter(parts):
    return [parts[0], send(parts[1], 1), send(parts[2], 2), send(parts[3], 3)]


def tie(first, *later):
    return lax.optimization_barrier((first, *later))


def body(
    act,
    cond,
    pair,
    pair_gain,
    chain_ids,
    bias_proj,
    chain_bias,
    cond_gain,
    ada_scale,
    ada_shift,
    qkvg,
    attn_out,
    out_gate,
    trans_in,
    trans_out,
):
    samples, rows, width = act.shape
    flat = samples * rows
    part = qkvg.shape[2]
    heads = part // HD
    act = act.reshape(flat, width)
    cond = cond.reshape(flat, cond.shape[2])
    w_proj = jnp.transpose(qkvg, (1, 2, 0))
    qkv, gates, cond_norm = project(act, cond, cond_gain, ada_scale, ada_shift, w_proj)
    qkv, pair = tie(qkv, pair)
    own = lax.all_to_all(qkv.reshape(8, 3 * HD, 4 * rows), "z", 0, 0, tiled=True)
    proj = jnp.transpose(bias_proj).reshape(4, heads, -1)
    tiles = tile_bias(pair, pair_gain, proj)
    spread = spread_bias(scatter(tiles), 8)
    win = trans_in.reshape(width, -1)
    own, spread, act, win = tie(own, spread, act, win)
    bias0 = lax.all_to_all(spread, "z", 0, 0, tiled=True)
    far = swap(own[:, HD:], "xh")
    *parts, g1 = transition(
        act, cond_norm, ada_scale, ada_shift, out_gate, win, trans_out, attn_out
    )
    bias0, g1 = tie(bias0, g1)
    parts = scatter(parts)
    bias2, far = tie(swap(bias0, "xlo"), far)
    bias1 = swap(bias0, "core")
    bias3 = swap(bias2, "core")
    quarter, pack = gated_sum(parts, g1)
    trans = around(quarter)
    w_out_all = [attn_out, pack, swap(pack, "core")]
    attended = attention(
        chain_bias, own, far, (bias0, bias1, bias2, bias3), chain_ids.reshape(8, 2 * rows)
    )
    attended = lax.all_to_all(attended, "z", 0, 0, tiled=True)
    updated = finish(around(mix(gates, attended)), w_out_all, cond_norm, out_gate, trans)
    return updated.reshape(samples, rows, width)


def solution(mesh):
    fine = jax.sharding.Mesh(
        mesh.devices.reshape(8, 2, 4, 2, 2), ("z", "xh", "col", "xlo", "core")
    )
    rows, groups = ("z", "xh"), ("xlo", "core")
    in_specs = (
        P(groups, rows, None),
        P(groups, rows, None),
        P(rows, ("col", *groups), None),
        P(),
        P(),
        P(),
        P(),
        P(),
        P(),
        P(),
        P(None, None, "col"),
        P("col", None),
        P(),
        P(None, None, "col"),
        P("col", None),
    )
    out_specs = P(groups, rows, None)
    return jax.shard_map(body, mesh=fine, in_specs=in_specs, out_specs=out_specs, check_vma=False)
```
